32 devices in a mesh: ctx: 8 (over z, x), ch: 4 (over y, core).
Axes of the slice: x: 2, y: 2, z: 4, core: 2. Of those that a mesh axis runs over, the one named last changes fastest.
Arguments:
- streams: bfloat16 [2048, 3, 4096], P('ctx', None, 'ch'), may hold values from -6 to 6
- feat_weight: float32 [3, 7, 4096], P(None, None, 'ch'), may hold values from -2 to 2
- skip_gain: float32 [4096], P('ch'), may hold values from -4 to 4
- spectrum_values: bfloat16 [2, 16, 256, 512], P(None, 'ctx', None, 'ch'), as said below
- spectrum_scales: float32 [16, 2, 512], P('ctx', None, 'ch'), may hold values from 0.25 to 4, as said below
- group_filter: int32 [256], replicated, may hold values from 0 to 511
- doc_lengths: int32 [32], replicated, may hold values from 1 to 512, 2048 in all
Outputs:
- mixed: bfloat16 [2048, 4096], P('ctx', 'ch')
The draws below stay inside these ranges and needn't reach their ends.
Inputs may be any that keep to these rules, and one draw needn't show every extreme that they name: `group_filter`: the filter index of each group of 16 neighbouring channels. `doc_lengths`: document lengths in sequence order, summing to 2048. `spectrum_values`: the spectra are those of real filters: the stored value at frequency 2 * 2048 - k is the complex conjugate of the value at k. `spectrum_scales`: frequencies k and 4096 - k have the same scale.
All inputs are finite; a program needn't handle non-finite values.
Results may differ from the reference program's by a relative error of at most 0.0085.
Values may be sent and summed in bfloat16 or wider, within the bound.
A program may use at most 64 MiB of HBM per device.

```python
import math
import jax
import jax.numpy as jnp
import numpy as np
from jax import lax

CHANNELS = 4096
GROUP_CH = 16
FILTERS = 512
FEAT_TAPS = 7
SCALE_BLOCK = 128
DOCS = 32
TOK_DEV = 256
SEQ = 2048
DOC_MOST = 512
GROUPS = 256
N_CTX = 8


def draw_spectrum_values(key, part):
    rows = 2 * N_CTX
    cols = TOK_DEV
    key_one, key_two = jax.random.split(key)
    first_draw = jax.random.truncated_normal(key_one, -6.0, 6.0, (rows, cols, FILTERS), jnp.float32)
    second_draw = jax.random.truncated_normal(key_two, -6.0, 6.0, (rows, cols, FILTERS), jnp.float32)
    row_index = jnp.arange(rows, dtype=jnp.int32)[:, None]
    col_index = jnp.arange(cols, dtype=jnp.int32)[None, :]
    row_mirror = jnp.where(row_index >= 2, jnp.bitwise_xor(row_index, 1), row_index) + 0 * col_index
    col_mirror = jnp.where(row_index == 0, (cols - col_index) % cols, cols - 1 - col_index)
    first_mirror = first_draw[row_mirror, col_mirror]
    second_mirror = second_draw[row_mirror, col_mirror]
    real_part = (first_draw + first_mirror) * 0.70710678
    imag_part = (second_draw - second_mirror) * 0.70710678
    return jnp.stack([real_part, imag_part]).astype(jnp.bfloat16)


def draw_spectrum_scales(key, part):
    rows = 2 * N_CTX
    blocks = TOK_DEV // SCALE_BLOCK
    base = jnp.exp(jax.random.uniform(key, (rows, blocks, FILTERS), jnp.float32, jnp.log(0.25), jnp.log(4.0)))
    row_index = jnp.arange(rows, dtype=jnp.int32)[:, None]
    block_index = jnp.arange(blocks, dtype=jnp.int32)[None, :]
    row_mirror = jnp.where(row_index >= 2, jnp.bitwise_xor(row_index, 1), row_index) + 0 * block_index
    block_mirror = blocks - 1 - block_index + 0 * row_index
    mirrored = base[row_mirror, block_mirror]
    paired = jnp.sqrt(base * mirrored)
    first_row = jnp.broadcast_to(base[0:1, 0:1, :], base.shape)
    chosen = jnp.where((row_index == 0)[:, :, None], first_row, paired)
    return jnp.clip(chosen, 0.25, 4.0).astype(jnp.float32)


def plant(values, rng, smallest, largest):
    index_at = [jax.random.randint(jax.random.fold_in(rng, axis), (), 0, length) for axis, length in enumerate(values.shape)]
    main_axis = values.shape.index(max(values.shape))
    beside = index_at[:main_axis] + [(index_at[main_axis] + 1) % values.shape[main_axis]] + index_at[main_axis + 1:]
    return values.at[tuple(index_at)].set(smallest).at[tuple(beside)].set(largest)


def level_of(stream_key, shape, cuts, low, top_value):
    loudness = 1.0
    for dim, shards_of in cuts:
        heights = jax.random.uniform(jax.random.fold_in(jax.random.fold_in(stream_key, 6), dim), (shards_of,), jnp.float32, low / len(cuts), top_value / len(cuts))
        loudness = loudness * jnp.repeat(jnp.exp(heights), shape[dim] // shards_of).reshape((-1,) + (1,) * (len(shape) - 1 - dim))
    return loudness


def length_profile(count, total, most, skew):
    loads = [(1 << 20) // math.isqrt(grade ** skew) + 1 for grade in range(2, count + 1)]
    rest, given = total - most - (count - 1), [1] * (count - 1)
    while rest > 0:
        candidates = [i for i in range(count - 1) if given[i] < most]
        pool, budget = sum([loads[i] for i in candidates]), rest
        for i in candidates:
            more = min(most - given[i], max(1, budget * loads[i] // pool), rest)
            given[i] = given[i] + more
            rest = rest - more
    return np.array([most] + given)


def ragged_sizes(key, number_of, total, most, slope):
    if number_of == 2:
        one = jax.random.randint(key, (), max(1, total - most), min(most, total - 1) + 1)
        return jnp.stack([one, total - one])
    tallies = jnp.asarray(length_profile(number_of, total, most, slope), jnp.int32)
    twos = (number_of - 1) // 2
    source_of, receiver = tallies[1:1 + 2 * twos:2], tallies[2:2 + 2 * twos:2]
    slack = jnp.minimum(source_of - 1, most - receiver)
    passed = jax.random.randint(jax.random.fold_in(key, 1), (twos,), 0, 1 << 20) % (slack + 1)
    tallies = tallies.at[1:1 + 2 * twos:2].set(source_of - passed).at[2:2 + 2 * twos:2].set(receiver + passed)
    return tallies[jax.random.permutation(jax.random.fold_in(key, 2), number_of)]


def noise(own_key, dims, scale, bound, cuts=(), held_as=jnp.bfloat16):
    loudness = level_of(own_key, dims, cuts, -0.22, 0.18) if cuts else 1.0
    result = jax.random.normal(own_key, dims, jnp.float32) * scale * loudness
    return jnp.minimum(jnp.maximum(result, -bound), bound).astype(held_as)


def setup_inputs(seed: int = 0) -> dict:
    arg_keys = jax.random.split(jax.random.key(seed), 8)
    streams = noise(arg_keys[0], (SEQ, 3, CHANNELS), 1.0, 6.0, ((0, 8), (2, 4)))
    feat_weight = noise(arg_keys[1], (3, FEAT_TAPS, CHANNELS), FEAT_TAPS ** -0.5, 2.0, ((2, 4),), jnp.float32)
    skip_gain = noise(arg_keys[2], (CHANNELS,), 1.0, 4.0, ((0, 4),), jnp.float32)
    spectrum_values = draw_spectrum_values(jax.random.fold_in(arg_keys[7], 71), 0)
    spectrum_scales = draw_spectrum_scales(jax.random.fold_in(arg_keys[7], 71), 0)
    group_filter = plant(jax.random.randint(arg_keys[5], (GROUPS,), 0, FILTERS), jax.random.fold_in(arg_keys[5], 1), 0, FILTERS - 1).astype(jnp.int32)
    doc_lengths = ragged_sizes(arg_keys[6], DOCS, SEQ, DOC_MOST, 2).astype(jnp.int32)
    return dict(streams=streams, feat_weight=feat_weight, skip_gain=skip_gain, spectrum_values=spectrum_values, spectrum_scales=spectrum_scales, group_filter=group_filter, doc_lengths=doc_lengths)


def row_order(twice_ctx):
    half = twice_ctx // 2
    table = np.zeros((twice_ctx,), np.int32)
    for device in range(half):
        table[device] = 2 * device
        partner = twice_ctx - device if device > 0 else half
        table[partner] = 2 * device + 1
    return table


def reference(streams, feat_weight, skip_gain, spectrum_values, spectrum_scales, group_filter, doc_lengths):
    seq = streams.shape[0]
    total_len = 2 * seq
    reach = FEAT_TAPS - 1
    ends = jnp.cumsum(doc_lengths)
    positions = jnp.arange(seq, dtype=jnp.int32)
    segment = jnp.sum((positions[:, None] >= ends[None, :]).astype(jnp.int32), axis=1)
    inputs = streams.astype(jnp.float32)
    padded = jnp.concatenate([jnp.zeros((reach,) + inputs.shape[1:], inputs.dtype), inputs], axis=0)
    seg_padded = jnp.concatenate([jnp.full((reach,), -1, jnp.int32), segment])
    featured = jnp.zeros(inputs.shape, jnp.float32)
    for tap_index in range(FEAT_TAPS):
        start = reach - tap_index
        source = padded[start:start + seq]
        same = (seg_padded[start:start + seq] == segment).astype(jnp.float32)
        featured = featured + feat_weight[:, tap_index, :][None] * source * same[:, None, None]
    query = featured[:, 0]
    mixed_in = featured[:, 1] * featured[:, 2]
    scale_full = jnp.repeat(spectrum_scales, SCALE_BLOCK, axis=1)
    bank = spectrum_values.astype(jnp.float32) * scale_full[None]
    order = jnp.asarray(row_order(2 * N_CTX))
    bank = jnp.take(bank, order, axis=1)
    natural = jnp.transpose(bank, (0, 2, 1, 3)).reshape(2, total_len, FILTERS)
    filter_of = jnp.repeat(group_filter, GROUP_CH)
    width = min(256, CHANNELS)
    count = CHANNELS // width

    def one_block(index):
        begin = (index * width).astype(jnp.int32)
        values = lax.dynamic_slice_in_dim(mixed_in, begin, width, 1)
        chosen = lax.dynamic_slice_in_dim(filter_of, begin, width, 0)
        spec = jnp.take(natural, chosen, axis=2)
        padded_vals = jnp.concatenate([values, jnp.zeros_like(values)], axis=0)
        freq = jnp.fft.fft(padded_vals, axis=0)
        prod = freq * lax.complex(spec[0], spec[1])
        return jnp.real(jnp.fft.ifft(prod, axis=0))[:seq]

    blocks = lax.map(one_block, jnp.arange(count, dtype=jnp.int32))
    conv = jnp.transpose(blocks, (1, 0, 2)).reshape(seq, CHANNELS)
    return (query * (conv + skip_gain[None] * mixed_in)).astype(jnp.bfloat16)
```

```python
import math

import jax
import jax.numpy as jnp
import numpy as np
from jax import lax
from jax.sharding import PartitionSpec as P

GROUP_CH = 16
FEAT_TAPS = 7
SCALE_BLOCK = 128


def from_behind(shard, axis, by):
    size = lax.axis_size(axis)
    pairs = [(i, i + by) for i in range(size) if 0 <= i + by < size]
    return lax.ppermute(shard, axis, pairs)


def wave(rows, cols, period):
    angle = np.outer(rows, cols) % period * (2.0 * math.pi / period)
    return np.cos(angle), np.sin(angle)


def featurize(streams, rim, feat_weight, doc_lengths, ctx_index):
    tokens = streams.shape[0]
    reach = FEAT_TAPS - 1
    extended = jnp.concatenate([rim, streams], axis=0).astype(jnp.float32)
    positions = ctx_index * tokens + jnp.arange(tokens, dtype=jnp.int32)
    ends = jnp.cumsum(doc_lengths)
    begins = jnp.max(jnp.where(positions[:, None] >= ends[None, :], ends[None, :], 0), axis=1)
    inside = positions - begins
    featured = jnp.zeros((tokens,) + streams.shape[1:], jnp.float32)
    for tap_index in range(FEAT_TAPS):
        start = reach - tap_index
        source = extended[start : start + tokens]
        same = inside >= tap_index
        featured = featured + jnp.where(
            same[:, None, None], feat_weight[:, tap_index, :][None] * source, 0.0
        )
    return featured[:, 0], featured[:, 1] * featured[:, 2]


def long_conv(columns, spec_real, spec_imag, ctx_count):
    tokens = columns.shape[1]
    total_len = 2 * tokens * ctx_count
    outer = np.arange(ctx_count + 1)
    cos_o, sin_o = wave(outer, np.arange(ctx_count), 2 * ctx_count)
    cos_t, sin_t = wave(outer, np.arange(tokens), total_len)
    cos_i, sin_i = wave(np.arange(tokens), np.arange(tokens), tokens)
    f32 = jnp.float32
    high = lax.Precision.HIGHEST
    xs = columns.astype(f32)
    u_real = jnp.einsum("ka,abc->kbc", jnp.asarray(cos_o, f32), xs, precision=high)
    u_imag = jnp.einsum("ka,abc->kbc", jnp.asarray(-sin_o, f32), xs, precision=high)
    ct, st = jnp.asarray(cos_t, f32)[:, :, None], jnp.asarray(sin_t, f32)[:, :, None]
    b_real = (u_real * ct + u_imag * st).astype(jnp.bfloat16)
    b_imag = (u_imag * ct - u_real * st).astype(jnp.bfloat16)
    table = jnp.asarray(np.concatenate([cos_i, sin_i], axis=0), jnp.bfloat16)

    def inner(real, imag):
        both = jnp.concatenate([real, imag], axis=2)
        out = jnp.einsum("qt,ktc->kqc", table, both, preferred_element_type=f32)
        width = real.shape[2]
        return (
            out[:, :tokens, :width],
            out[:, :tokens, width:],
            out[:, tokens:, :width],
            out[:, tokens:, width:],
        )

    cr, ci, sr, si = inner(b_real, b_imag)
    z_real, z_imag = cr + si, ci - sr
    p_real = (z_real * spec_real - z_imag * spec_imag).astype(jnp.bfloat16)
    p_imag = (z_real * spec_imag + z_imag * spec_real).astype(jnp.bfloat16)
    cr, ci, sr, si = inner(p_real, p_imag)
    v_real, v_imag = cr - si, ci + sr
    t_real = v_real * ct - v_imag * st
    t_imag = v_imag * ct + v_real * st
    weight = np.where((outer == 0) | (outer == ctx_count), 1.0, 2.0)[:, None] / total_len
    back_r = jnp.asarray(cos_o * weight, f32)
    back_i = jnp.asarray(-sin_o * weight, f32)
    return jnp.einsum("ka,kbc->abc", back_r, t_real, precision=high) + jnp.einsum(
        "ka,kbc->abc", back_i, t_imag, precision=high
    )


def per_device(
    streams, feat_weight, skip_gain, spectrum_values, spectrum_scales, group_filter, doc_lengths
):
    tokens = streams.shape[0]
    local_ch = streams.shape[2]
    ctx_count = lax.axis_size("ctx")
    reach = FEAT_TAPS - 1
    ctx_index = lax.axis_index("ctx")
    ch_index = lax.axis_index("ch")
    groups_local = local_ch // GROUP_CH
    scaled = spectrum_values.astype(jnp.float32) * jnp.repeat(spectrum_scales, SCALE_BLOCK, axis=1)
    bank = lax.all_gather(scaled.astype(jnp.bfloat16), "ch", axis=3, tiled=True)
    mine = lax.dynamic_slice_in_dim(group_filter, ch_index * groups_local, groups_local)
    onehot = jnp.arange(bank.shape[3], dtype=jnp.int32)[:, None] == mine[None, :]
    chosen = jnp.einsum(
        "rkqf,fg->kgrq", bank, onehot.astype(jnp.bfloat16), preferred_element_type=jnp.float32
    ).astype(jnp.bfloat16)
    rim = from_behind(streams[tokens - reach :], "ctx", 1)
    query, mixed_in = featurize(streams, rim, feat_weight, doc_lengths, ctx_index)
    columns = lax.all_to_all(
        mixed_in.astype(jnp.bfloat16), "ctx", split_axis=1, concat_axis=0, tiled=True
    ).reshape(ctx_count, tokens, -1)
    spec = lax.all_to_all(chosen, "ctx", split_axis=1, concat_axis=0, tiled=True)
    spec = jnp.concatenate([spec[0::2], spec[1:2]], axis=0)
    spec = jnp.repeat(jnp.transpose(spec, (2, 0, 3, 1)), GROUP_CH, axis=3).astype(jnp.float32)
    signal = long_conv(columns, spec[0], spec[1], ctx_count)
    conv = lax.all_to_all(
        signal.astype(jnp.bfloat16), "ctx", split_axis=0, concat_axis=2, tiled=True
    ).reshape(tokens, local_ch)
    conv = conv.astype(jnp.float32)
    return (query * (conv + skip_gain[None] * mixed_in)).astype(jnp.bfloat16)


def solution(mesh):
    placed = (
        P("ctx", None, "ch"),
        P(None, None, "ch"),
        P("ch"),
        P(None, "ctx", None, "ch"),
        P("ctx", None, "ch"),
        P(),
        P(),
    )
    return jax.shard_map(
        per_device, mesh=mesh, in_specs=placed, out_specs=P("ctx", "ch"), check_vma=False
    )
```

```python
import functools
import math

import jax
import jax.numpy as jnp
import numpy as np
from jax import lax
from jax.experimental import pallas as pl
from jax.experimental.pallas import tpu as pltpu
from jax.sharding import PartitionSpec as P

GROUP_CH = 16
FEAT_TAPS = 7
SCALE_BLOCK = 128


def from_behind(shard, axis, by):
    size = lax.axis_size(axis)
    pairs = [(i, i + by) for i in range(size) if 0 <= i + by < size]
    return lax.ppermute(shard, axis, pairs)


def wave(rows, cols, period):
    angle = np.outer(rows, cols) % period * (2.0 * math.pi / period)
    return np.cos(angle), np.sin(angle)


def featurize(streams, rim, feat_weight, doc_lengths, ctx_index):
    tokens = streams.shape[0]
    reach = FEAT_TAPS - 1
    extended = jnp.concatenate([rim, streams], axis=0).astype(jnp.float32)
    positions = ctx_index * tokens + jnp.arange(tokens, dtype=jnp.int32)
    ends = jnp.cumsum(doc_lengths)
    begins = jnp.max(jnp.where(positions[:, None] >= ends[None, :], ends[None, :], 0), axis=1)
    inside = positions - begins
    featured = jnp.zeros((tokens,) + streams.shape[1:], jnp.float32)
    for tap_index in range(FEAT_TAPS):
        start = reach - tap_index
        source = extended[start : start + tokens]
        same = inside >= tap_index
        featured = featured + jnp.where(
            same[:, None, None], feat_weight[:, tap_index, :][None] * source, 0.0
        )
    return featured[:, 0], featured[:, 1] * featured[:, 2]


def long_conv(columns, spec_real, spec_imag, ctx_count):
    tokens = columns.shape[1]
    total_len = 2 * tokens * ctx_count
    outer = np.arange(ctx_count + 1)
    cos_o, sin_o = wave(outer, np.arange(ctx_count), 2 * ctx_count)
    cos_t, sin_t = wave(outer, np.arange(tokens), total_len)
    cos_i, sin_i = wave(np.arange(tokens), np.arange(tokens), tokens)
    f32 = jnp.float32
    high = lax.Precision.HIGHEST
    xs = columns.astype(f32)
    u_real = jnp.einsum("ka,abc->kbc", jnp.asarray(cos_o, f32), xs, precision=high)
    u_imag = jnp.einsum("ka,abc->kbc", jnp.asarray(-sin_o, f32), xs, precision=high)
    ct, st = jnp.asarray(cos_t, f32)[:, :, None], jnp.asarray(sin_t, f32)[:, :, None]
    b_real = (u_real * ct + u_imag * st).astype(jnp.bfloat16)
    b_imag = (u_imag * ct - u_real * st).astype(jnp.bfloat16)
    table = jnp.asarray(np.concatenate([cos_i, sin_i], axis=0), jnp.bfloat16)

    def inner(real, imag):
        both = jnp.concatenate([real, imag], axis=2)
        out = jnp.einsum("qt,ktc->kqc", table, both, preferred_element_type=f32)
        width = real.shape[2]
        return (
            out[:, :tokens, :width],
            out[:, :tokens, width:],
            out[:, tokens:, :width],
            out[:, tokens:, width:],
        )

    cr, ci, sr, si = inner(b_real, b_imag)
    z_real, z_imag = cr + si, ci - sr
    p_real = (z_real * spec_real - z_imag * spec_imag).astype(jnp.bfloat16)
    p_imag = (z_real * spec_imag + z_imag * spec_real).astype(jnp.bfloat16)
    cr, ci, sr, si = inner(p_real, p_imag)
    v_real, v_imag = cr - si, ci + sr
    t_real = v_real * ct - v_imag * st
    t_imag = v_imag * ct + v_real * st
    weight = np.where((outer == 0) | (outer == ctx_count), 1.0, 2.0)[:, None] / total_len
    back_r = jnp.asarray(cos_o * weight, f32)
    back_i = jnp.asarray(-sin_o * weight, f32)
    return jnp.einsum("ka,kbc->abc", back_r, t_real, precision=high) + jnp.einsum(
        "ka,kbc->abc", back_i, t_imag, precision=high
    )


def by_collectives(
    streams, feat_weight, skip_gain, spectrum_values, spectrum_scales, group_filter, doc_lengths
):
    tokens = streams.shape[0]
    local_ch = streams.shape[2]
    ctx_count = lax.axis_size("ctx")
    reach = FEAT_TAPS - 1
    ctx_index = lax.axis_index("ctx")
    ch_index = lax.axis_index("ch")
    groups_local = local_ch // GROUP_CH
    scaled = spectrum_values.astype(jnp.float32) * jnp.repeat(spectrum_scales, SCALE_BLOCK, axis=1)
    bank = lax.all_gather(scaled.astype(jnp.bfloat16), "ch", axis=3, tiled=True)
    mine = lax.dynamic_slice_in_dim(group_filter, ch_index * groups_local, groups_local)
    onehot = jnp.arange(bank.shape[3], dtype=jnp.int32)[:, None] == mine[None, :]
    chosen = jnp.einsum(
        "rkqf,fg->kgrq", bank, onehot.astype(jnp.bfloat16), preferred_element_type=jnp.float32
    ).astype(jnp.bfloat16)
    rim = from_behind(streams[tokens - reach :], "ctx", 1)
    query, mixed_in = featurize(streams, rim, feat_weight, doc_lengths, ctx_index)
    columns = lax.all_to_all(
        mixed_in.astype(jnp.bfloat16), "ctx", split_axis=1, concat_axis=0, tiled=True
    ).reshape(ctx_count, tokens, -1)
    spec = lax.all_to_all(chosen, "ctx", split_axis=1, concat_axis=0, tiled=True)
    spec = jnp.concatenate([spec[0::2], spec[1:2]], axis=0)
    spec = jnp.repeat(jnp.transpose(spec, (2, 0, 3, 1)), GROUP_CH, axis=3).astype(jnp.float32)
    signal = long_conv(columns, spec[0], spec[1], ctx_count)
    conv = lax.all_to_all(
        signal.astype(jnp.bfloat16), "ctx", split_axis=0, concat_axis=2, tiled=True
    ).reshape(tokens, local_ch)
    conv = conv.astype(jnp.float32)
    return (query * (conv + skip_gain[None] * mixed_in)).astype(jnp.bfloat16)


LANES = 128


def block_kernel(
    ctx_count, ch_count,
    streams, inside, taps, gain, values, scales, onehot, spread, dft_hbm, twist_hbm,
    out,
    dft, twist, ext, rim, chosen, bank, mine, spec, keep, query, sends, columns,
    inner_in, inner_out, signal, back,
    table_sem, rim_sem, ch_send, ch_recv, spec_send, spec_recv, last_send, last_recv,
    go_send, go_recv, back_send, back_recv,
):
    f32, bf16 = jnp.float32, jnp.bfloat16
    tokens = streams.shape[1]
    me = lax.axis_index("ctx")
    my_ch = lax.axis_index("ch")
    total_len = 2 * tokens * ctx_count

    def remote(src, dst, send, recv, ctx_to, ch_to):
        return pltpu.make_async_remote_copy(
            src_ref=src, dst_ref=dst, send_sem=send, recv_sem=recv,
            device_id=(ctx_to, ch_to), device_id_type=pl.DeviceIdType.MESH,
        )

    def ctx_at(step):
        return lax.rem(me + step, ctx_count)

    def ch_at(step):
        return lax.rem(my_ch + step, ch_count)

    load_dft = pltpu.make_async_copy(dft_hbm, dft, table_sem.at[0])
    load_twist = pltpu.make_async_copy(twist_hbm, twist, table_sem.at[1])
    load_dft.start()
    load_twist.start()

    barrier = pltpu.get_barrier_semaphore()
    for step in range(1, ctx_count):
        pl.semaphore_signal(
            barrier, inc=1, device_id=(ctx_at(step), my_ch), device_id_type=pl.DeviceIdType.MESH
        )
    for step in range(1, ch_count):
        pl.semaphore_signal(
            barrier, inc=1, device_id=(me, ch_at(step)), device_id_type=pl.DeviceIdType.MESH
        )
    pl.semaphore_wait(barrier, ctx_count + ch_count - 2)

    send_rim = remote(
        streams.at[:, pl.ds(tokens - 16, 16), :], rim, rim_sem.at[0], rim_sem.at[1],
        ctx_at(1), my_ch,
    )
    send_rim.start()

    halves = tokens // SCALE_BLOCK
    for row in range(2):
        parts = []
        for part in range(2):
            bands = []
            for half in range(halves):
                band = values[part, row, half * SCALE_BLOCK : (half + 1) * SCALE_BLOCK, :]
                bands.append(band.astype(f32) * scales[row, half : half + 1, :])
            scaled = jnp.concatenate(bands, axis=0).astype(bf16)
            parts.append(
                lax.dot_general(
                    onehot[...], scaled, (((1,), (1,)), ((), ())), preferred_element_type=f32
                )
            )
        for h in range(ch_count):
            for c in range(ctx_count):
                at = (h * ctx_count + c) * 8
                chosen[h, row, c] = jnp.concatenate(
                    [parts[0][at : at + 8], parts[1][at : at + 8]], axis=0
                ).astype(bf16)

    def ch_copy(step):
        to = ch_at(step)
        return remote(
            chosen.at[to], bank.at[my_ch], ch_send.at[step], ch_recv.at[step], me, to
        )

    for step in range(1, ch_count):
        ch_copy(step).start()

    send_rim.wait()
    chunk = 64

    def feature(stream, lanes, store):
        ext[0:8, :] = rim[stream, :, lanes].astype(f32)[8:16]
        ext[8 : 8 + tokens, :] = streams[stream, :, lanes].astype(f32)
        for at in range(0, tokens, chunk):
            where_in = inside[at : at + chunk, :]
            total = jnp.zeros((chunk, LANES), f32)
            for tap in range(FEAT_TAPS):
                index = stream * FEAT_TAPS + tap
                term = taps[index : index + 1, lanes] * ext[at + 8 - tap : at + 8 - tap + chunk, :]
                if tap:
                    term = jnp.where(where_in >= tap, term, 0.0)
                total = total + term
            store(at, total)

    def product(block):
        lanes = pl.ds(pl.multiple_of(block * LANES, LANES), LANES)

        def put_key(at, total):
            keep[block, at : at + chunk, :] = total

        def put_product(at, total):
            both = keep[block, at : at + chunk, :] * total
            keep[block, at : at + chunk, :] = both
            sends[block, at : at + chunk, :] = both.astype(bf16)

        feature(1, lanes, put_key)
        feature(2, lanes, put_product)

    def order(index):
        return 1 + lax.rem(index + 3, ctx_count - 1)

    def go_copy(step):
        to = ctx_at(step)
        return remote(sends.at[to], columns.at[me], go_send.at[step], go_recv.at[step], to, my_ch)

    def go(index, carry):
        step = order(index)
        product(ctx_at(step))
        go_copy(step).start()
        return carry

    lax.fori_loop(0, ctx_count - 1, go, 0)
    product(me)
    columns[me] = sends[me]

    for step in range(1, ch_count):
        ch_copy(step).wait()
    bank[my_ch] = chosen[my_ch]
    for row in range(2):
        for c in range(ctx_count):
            total = bank[0, row, c].astype(f32)
            for h in range(1, ch_count):
                total = total + bank[h, row, c].astype(f32)
            mine[row, c] = total.astype(bf16)

    def spec_copy(step):
        to = ctx_at(step)
        return remote(
            mine.at[0, to], spec.at[me], spec_send.at[step], spec_recv.at[step], to, my_ch
        )

    def last_copy(step):
        return remote(
            mine.at[1, step], spec.at[ctx_count], last_send.at[step], last_recv.at[0], step, my_ch
        )

    for step in range(1, ctx_count):
        spec_copy(step).start()
    spec[me] = mine[0, me]

    @pl.when(me == 0)
    def _():
        for step in range(1, ctx_count):
            last_copy(step).start()
        spec[ctx_count] = mine[1, 0]

    def ask(block, carry):
        lanes = pl.ds(pl.multiple_of(block * LANES, LANES), LANES)

        def put_query(at, total):
            query[block, at : at + chunk, :] = total

        feature(0, lanes, put_query)
        return carry

    lax.fori_loop(0, ctx_count, ask, 0)

    load_dft.wait()
    load_twist.wait()
    for step in range(1, ctx_count):
        spec_copy(step).wait()

    @pl.when(me == 0)
    def _():
        for step in range(1, ctx_count):
            last_copy(step).wait_send()

    @pl.when(me != 0)
    def _():
        last_copy(1).wait_recv()

    for step in range(1, ctx_count):
        go_copy(step).wait()

    half = ctx_count // 2
    rows = 16

    def co(a, k):
        return math.cos(math.pi * (a * k % (2 * ctx_count)) / ctx_count)

    def si(a, k):
        return math.sin(math.pi * (a * k % (2 * ctx_count)) / ctx_count)

    def gather(terms, coefs):
        total = None
        for term, coef in zip(terms, coefs):
            if abs(coef) < 1e-9:
                continue
            if abs(coef - 1) < 1e-9:
                piece = term
            elif abs(coef + 1) < 1e-9:
                piece = -term
            else:
                piece = term * coef
            total = piece if total is None else total + piece
        return jnp.zeros_like(terms[0]) if total is None else total

    def outer_step(index, carry):
        at = pl.ds(pl.multiple_of(index * rows, rows), rows)
        x = [columns[a, at, :].astype(f32) for a in range(ctx_count)]
        even, odd = list(range(0, ctx_count, 2)), list(range(1, ctx_count, 2))

        def put(k, real, imag):
            c, s = twist[k, 0, at, :], twist[k, 1, at, :]
            inner_in[k, at, 0:LANES] = (real * c + imag * s).astype(bf16)
            inner_in[k, at, LANES : 2 * LANES] = (imag * c - real * s).astype(bf16)

        for k in range(half + 1):
            ce = gather([x[a] for a in even], [co(a, k) for a in even])
            cd = gather([x[a] for a in odd], [co(a, k) for a in odd])
            se = gather([x[a] for a in even], [si(a, k) for a in even])
            sd = gather([x[a] for a in odd], [si(a, k) for a in odd])
            put(k, ce + cd, -(se + sd))
            if k != ctx_count - k:
                put(ctx_count - k, ce - cd, se - sd)
        return carry

    lax.fori_loop(0, tokens // rows, outer_step, 0)

    def inner(both):
        result = jnp.dot(dft[...], both, preferred_element_type=f32)
        return (
            result[:tokens, :LANES], result[:tokens, LANES:],
            result[tokens:, :LANES], result[tokens:, LANES:],
        )

    def row_step(k, carry):
        picked = spec[k].astype(f32).T.astype(bf16)
        wide = jnp.dot(picked, spread[...], preferred_element_type=f32)
        s_real, s_imag = wide[:, :LANES], wide[:, LANES:]
        cr, ci, sr, sj = inner(inner_in[k])
        z_real, z_imag = cr + sj, ci - sr
        p_real = (z_real * s_real - z_imag * s_imag).astype(bf16)
        p_imag = (z_real * s_imag + z_imag * s_real).astype(bf16)
        cr, ci, sr, sj = inner(jnp.concatenate([p_real, p_imag], axis=1))
        v_real, v_imag = cr - sj, ci + sr
        c, s = twist[k, 0], twist[k, 1]
        inner_out[k, 0] = v_real * c - v_imag * s
        inner_out[k, 1] = v_imag * c + v_real * s
        return carry

    lax.fori_loop(0, ctx_count + 1, row_step, 0)

    def last_step(index, carry):
        at = pl.ds(pl.multiple_of(index * rows, rows), rows)
        real = [inner_out[k, 0, at, :] for k in range(ctx_count + 1)]
        imag = [inner_out[k, 1, at, :] for k in range(ctx_count + 1)]
        for parity in range(2):
            sign = 1.0 if parity == 0 else -1.0
            folded_r = [real[k] + sign * real[ctx_count - k] for k in range(half)] + [real[half]]
            folded_i = [imag[k] - sign * imag[ctx_count - k] for k in range(half)] + [imag[half]]
            for a in range(parity, ctx_count, 2):
                weights = [(1.0 if k == 0 else 2.0) for k in range(half + 1)]
                total = gather(
                    folded_r + folded_i,
                    [w * co(a, k) for k, w in enumerate(weights)]
                    + [-w * si(a, k) for k, w in enumerate(weights)],
                )
                signal[a, at, :] = (total * (1.0 / total_len)).astype(bf16)
        return carry

    lax.fori_loop(0, tokens // rows, last_step, 0)

    def back_copy(step):
        to = ctx_at(step)
        return remote(signal.at[to], back.at[me], back_send.at[step], back_recv.at[step], to, my_ch)

    def send_back(index, carry):
        back_copy(order(index)).start()
        return carry

    lax.fori_loop(0, ctx_count - 1, send_back, 0)

    def finish(block, conv):
        lanes = pl.ds(pl.multiple_of(block * LANES, LANES), LANES)
        skipped = gain[0:1, lanes] * keep[block]
        out[:, lanes] = (query[block] * (conv.astype(f32) + skipped)).astype(bf16)

    finish(me, signal[me])

    def receive(index, carry):
        step = order(index)
        back_copy(step).wait()
        source = lax.rem(me + ctx_count - step, ctx_count)
        finish(source, back[source])
        return carry

    lax.fori_loop(0, ctx_count - 1, receive, 0)


def fused(streams, inside, feat_weight, skip_gain, spectrum_values, spectrum_scales, onehot):
    ctx_count, ch_count = lax.axis_size("ctx"), lax.axis_size("ch")
    tokens, _, local_ch = streams.shape
    rows = ctx_count + 1
    f32, bf16 = jnp.float32, jnp.bfloat16
    cos_t, sin_t = wave(np.arange(rows), np.arange(tokens), 2 * tokens * ctx_count)
    twist = np.stack([cos_t, sin_t], axis=1).astype(np.float32)[..., None]
    twist = np.ascontiguousarray(np.broadcast_to(twist, twist.shape[:3] + (LANES,)))
    cos_i, sin_i = wave(np.arange(tokens), np.arange(tokens), tokens)
    dft = jnp.asarray(np.concatenate([cos_i, sin_i], axis=0), bf16)
    owner = np.arange(2 * LANES) % LANES // GROUP_CH + 8 * (np.arange(2 * LANES) // LANES)
    spread = jnp.asarray(np.arange(16)[:, None] == owner[None, :], bf16)
    vmem = pl.BlockSpec(memory_space=pltpu.VMEM)
    hbm = pl.BlockSpec(memory_space=pl.ANY)
    dma = lambda count: pltpu.SemaphoreType.DMA((count,))
    block = (ctx_count, tokens, LANES)
    picks = (2, ctx_count, 16, tokens)
    return pl.pallas_call(
        functools.partial(block_kernel, ctx_count, ch_count),
        out_shape=jax.ShapeDtypeStruct((tokens, local_ch), bf16),
        in_specs=[vmem] * 8 + [hbm] * 2,
        out_specs=vmem,
        scratch_shapes=[
            pltpu.VMEM((2 * tokens, tokens), bf16),
            pltpu.VMEM((rows, 2, tokens, LANES), f32),
            pltpu.VMEM((tokens + 8, LANES), f32),
            pltpu.VMEM((3, 16, local_ch), bf16),
            pltpu.VMEM((ch_count,) + picks, bf16),
            pltpu.VMEM((ch_count,) + picks, bf16),
            pltpu.VMEM(picks, bf16),
            pltpu.VMEM((rows, 16, tokens), bf16),
            pltpu.VMEM(block, f32),
            pltpu.VMEM(block, f32),
            pltpu.VMEM(block, bf16),
            pltpu.VMEM(block, bf16),
            pltpu.VMEM((rows, tokens, 2 * LANES), bf16),
            pltpu.VMEM((rows, 2, tokens, LANES), f32),
            pltpu.VMEM(block, bf16),
            pltpu.VMEM(block, bf16),
            dma(2), dma(2), dma(ch_count), dma(ch_count), dma(ctx_count), dma(ctx_count),
            dma(ctx_count), dma(1), dma(ctx_count), dma(ctx_count), dma(ctx_count), dma(ctx_count),
        ],
        compiler_params=pltpu.CompilerParams(
            collective_id=0, has_side_effects=True, vmem_limit_bytes=40 * 2**20
        ),
    )(
        jnp.transpose(streams, (1, 0, 2)), inside, feat_weight.reshape(-1, local_ch),
        skip_gain[None], spectrum_values, spectrum_scales, onehot, spread, dft,
        jnp.asarray(twist),
    )


def per_device(
    streams, feat_weight, skip_gain, spectrum_values, spectrum_scales, group_filter, doc_lengths
):
    tokens, _, local_ch = streams.shape
    filters = spectrum_values.shape[3]
    if local_ch != lax.axis_size("ctx") * LANES or filters % LANES or tokens % SCALE_BLOCK:
        return by_collectives(
            streams, feat_weight, skip_gain, spectrum_values, spectrum_scales, group_filter,
            doc_lengths,
        )
    positions = lax.axis_index("ctx") * tokens + jnp.arange(tokens, dtype=jnp.int32)
    ends = jnp.cumsum(doc_lengths)
    begins = jnp.max(jnp.where(positions[:, None] >= ends[None, :], ends[None, :], 0), axis=1)
    inside = jnp.broadcast_to((positions - begins)[:, None], (tokens, LANES))
    held = lax.axis_index("ch") * filters + jnp.arange(filters, dtype=jnp.int32)
    onehot = (group_filter[:, None] == held[None, :]).astype(jnp.bfloat16)
    return fused(
        streams, inside, feat_weight, skip_gain, spectrum_values, spectrum_scales, onehot
    )


def solution(mesh):
    placed = (
        P("ctx", None, "ch"),
        P(None, None, "ch"),
        P("ch"),
        P(None, "ctx", None, "ch"),
        P("ctx", None, "ch"),
        P(),
        P(),
    )
    return jax.shard_map(
        per_device, mesh=mesh, in_specs=placed, out_specs=P("ctx", "ch"), check_vma=False
    )
```

```python
import functools
import math

import jax
import jax.numpy as jnp
import numpy as np
from jax import lax
from jax.experimental import pallas as pl
from jax.experimental.pallas import tpu as pltpu
from jax.sharding import PartitionSpec as P

GROUP_CH = 16
FEAT_TAPS = 7
SCALE_BLOCK = 128


def from_behind(shard, axis, by):
    size = lax.axis_size(axis)
    pairs = [(i, i + by) for i in range(size) if 0 <= i + by < size]
    return lax.ppermute(shard, axis, pairs)


def wave(rows, cols, period):
    angle = np.outer(rows, cols) % period * (2.0 * math.pi / period)
    return np.cos(angle), np.sin(angle)


def featurize(streams, rim, feat_weight, doc_lengths, ctx_index):
    tokens = streams.shape[0]
    reach = FEAT_TAPS - 1
    extended = jnp.concatenate([rim, streams], axis=0).astype(jnp.float32)
    positions = ctx_index * tokens + jnp.arange(tokens, dtype=jnp.int32)
    ends = jnp.cumsum(doc_lengths)
    begins = jnp.max(jnp.where(positions[:, None] >= ends[None, :], ends[None, :], 0), axis=1)
    inside = positions - begins
    featured = jnp.zeros((tokens,) + streams.shape[1:], jnp.float32)
    for tap_index in range(FEAT_TAPS):
        start = reach - tap_index
        source = extended[start : start + tokens]
        same = inside >= tap_index
        featured = featured + jnp.where(
            same[:, None, None], feat_weight[:, tap_index, :][None] * source, 0.0
        )
    return featured[:, 0], featured[:, 1] * featured[:, 2]


def long_conv(columns, spec_real, spec_imag, ctx_count):
    tokens = columns.shape[1]
    total_len = 2 * tokens * ctx_count
    outer = np.arange(ctx_count + 1)
    cos_o, sin_o = wave(outer, np.arange(ctx_count), 2 * ctx_count)
    cos_t, sin_t = wave(outer, np.arange(tokens), total_len)
    cos_i, sin_i = wave(np.arange(tokens), np.arange(tokens), tokens)
    f32 = jnp.float32
    high = lax.Precision.HIGHEST
    xs = columns.astype(f32)
    u_real = jnp.einsum("ka,abc->kbc", jnp.asarray(cos_o, f32), xs, precision=high)
    u_imag = jnp.einsum("ka,abc->kbc", jnp.asarray(-sin_o, f32), xs, precision=high)
    ct, st = jnp.asarray(cos_t, f32)[:, :, None], jnp.asarray(sin_t, f32)[:, :, None]
    b_real = (u_real * ct + u_imag * st).astype(jnp.bfloat16)
    b_imag = (u_imag * ct - u_real * st).astype(jnp.bfloat16)
    table = jnp.asarray(np.concatenate([cos_i, sin_i], axis=0), jnp.bfloat16)

    def inner(real, imag):
        both = jnp.concatenate([real, imag], axis=2)
        out = jnp.einsum("qt,ktc->kqc", table, both, preferred_element_type=f32)
        width = real.shape[2]
        return (
            out[:, :tokens, :width],
            out[:, :tokens, width:],
            out[:, tokens:, :width],
            out[:, tokens:, width:],
        )

    cr, ci, sr, si = inner(b_real, b_imag)
    z_real, z_imag = cr + si, ci - sr
    p_real = (z_real * spec_real - z_imag * spec_imag).astype(jnp.bfloat16)
    p_imag = (z_real * spec_imag + z_imag * spec_real).astype(jnp.bfloat16)
    cr, ci, sr, si = inner(p_real, p_imag)
    v_real, v_imag = cr - si, ci + sr
    t_real = v_real * ct - v_imag * st
    t_imag = v_imag * ct + v_real * st
    weight = np.where((outer == 0) | (outer == ctx_count), 1.0, 2.0)[:, None] / total_len
    back_r = jnp.asarray(cos_o * weight, f32)
    back_i = jnp.asarray(-sin_o * weight, f32)
    return jnp.einsum("ka,kbc->abc", back_r, t_real, precision=high) + jnp.einsum(
        "ka,kbc->abc", back_i, t_imag, precision=high
    )


def by_collectives(
    streams, feat_weight, skip_gain, spectrum_values, spectrum_scales, group_filter, doc_lengths
):
    tokens = streams.shape[0]
    local_ch = streams.shape[2]
    ctx_count = lax.axis_size("ctx")
    reach = FEAT_TAPS - 1
    ctx_index = lax.axis_index("ctx")
    ch_index = lax.axis_index("ch")
    groups_local = local_ch // GROUP_CH
    scaled = spectrum_values.astype(jnp.float32) * jnp.repeat(spectrum_scales, SCALE_BLOCK, axis=1)
    bank = lax.all_gather(scaled.astype(jnp.bfloat16), "ch", axis=3, tiled=True)
    mine = lax.dynamic_slice_in_dim(group_filter, ch_index * groups_local, groups_local)
    onehot = jnp.arange(bank.shape[3], dtype=jnp.int32)[:, None] == mine[None, :]
    chosen = jnp.einsum(
        "rkqf,fg->kgrq", bank, onehot.astype(jnp.bfloat16), preferred_element_type=jnp.float32
    ).astype(jnp.bfloat16)
    rim = from_behind(streams[tokens - reach :], "ctx", 1)
    query, mixed_in = featurize(streams, rim, feat_weight, doc_lengths, ctx_index)
    columns = lax.all_to_all(
        mixed_in.astype(jnp.bfloat16), "ctx", split_axis=1, concat_axis=0, tiled=True
    ).reshape(ctx_count, tokens, -1)
    spec = lax.all_to_all(chosen, "ctx", split_axis=1, concat_axis=0, tiled=True)
    spec = jnp.concatenate([spec[0::2], spec[1:2]], axis=0)
    spec = jnp.repeat(jnp.transpose(spec, (2, 0, 3, 1)), GROUP_CH, axis=3).astype(jnp.float32)
    signal = long_conv(columns, spec[0], spec[1], ctx_count)
    conv = lax.all_to_all(
        signal.astype(jnp.bfloat16), "ctx", split_axis=0, concat_axis=2, tiled=True
    ).reshape(tokens, local_ch)
    conv = conv.astype(jnp.float32)
    return (query * (conv + skip_gain[None] * mixed_in)).astype(jnp.bfloat16)


LANES = 128


def block_kernel(
    ctx_count, ch_count,
    streams_hbm, lengths, taps_hbm, gain_hbm, values_hbm, scales_hbm, groups_hbm, dft_hbm,
    twist_hbm,
    out,
    streams, inside, taps, gain, values, scales, groups, dft_wide, dft, twist, wide, ext, rim, chosen, bank, mine, spec, keep, query, sends, columns,
    inner_in, inner_out, signal, back,
    table_sem, rim_sem, ch_send, ch_recv, spec_send, spec_recv, last_send, last_recv,
    go_send, go_recv, back_send, back_recv,
):
    f32, bf16 = jnp.float32, jnp.bfloat16
    tokens = streams_hbm.shape[1]
    me = lax.axis_index("ctx")
    my_ch = lax.axis_index("ch")
    total_len = 2 * tokens * ctx_count

    def remote(src, dst, send, recv, ctx_to, ch_to):
        return pltpu.make_async_remote_copy(
            src_ref=src, dst_ref=dst, send_sem=send, recv_sem=recv,
            device_id=(ctx_to, ch_to), device_id_type=pl.DeviceIdType.MESH,
        )

    def ctx_at(step):
        return lax.rem(me + step, ctx_count)

    def ch_at(step):
        return lax.rem(my_ch + step, ch_count)

    loads = [
        pltpu.make_async_copy(source, target, table_sem.at[index])
        for index, (source, target) in enumerate(
            [
                (values_hbm, values), (scales_hbm, scales), (groups_hbm, groups),
                (taps_hbm, taps), (streams_hbm, streams),
                (gain_hbm, gain), (dft_hbm, dft_wide), (twist_hbm, twist),
            ]
        )
    ]
    for load in loads:
        load.start()

    barrier = pltpu.get_barrier_semaphore()
    for step in range(1, ctx_count):
        pl.semaphore_signal(
            barrier, inc=1, device_id=(ctx_at(step), my_ch), device_id_type=pl.DeviceIdType.MESH
        )
    for step in range(1, ch_count):
        pl.semaphore_signal(
            barrier, inc=1, device_id=(me, ch_at(step)), device_id_type=pl.DeviceIdType.MESH
        )

    for load in loads[:3]:
        load.wait()
    filters = values.shape[3]
    held = my_ch * filters + lax.broadcasted_iota(jnp.int32, (filters, groups.shape[1]), 0)
    onehot = jnp.where(held == groups[...], 1.0, 0.0).astype(f32).T.astype(bf16)
    halves = tokens // SCALE_BLOCK
    for row in range(2):
        parts = []
        for part in range(2):
            bands = []
            for half in range(halves):
                band = values[part, row, half * SCALE_BLOCK : (half + 1) * SCALE_BLOCK, :]
                bands.append(band.astype(f32) * scales[row, half : half + 1, :])
            scaled = jnp.concatenate(bands, axis=0).astype(bf16)
            parts.append(
                lax.dot_general(
                    onehot, scaled, (((1,), (1,)), ((), ())), preferred_element_type=f32
                )
            )
        for h in range(ch_count):
            for c in range(ctx_count):
                at = (h * ctx_count + c) * 8
                chosen[h, row, c] = jnp.concatenate(
                    [parts[0][at : at + 8], parts[1][at : at + 8]], axis=0
                ).astype(bf16)

    begins = jnp.zeros((tokens, LANES), jnp.int32)
    places = me * tokens + lax.broadcasted_iota(jnp.int32, (tokens, LANES), 0)
    end = jnp.int32(0)
    for doc in range(lengths.shape[0]):
        end = end + lengths[doc]
        begins = jnp.where(places >= end, end, begins)
    inside[...] = places - begins

    pl.semaphore_wait(barrier, ctx_count + ch_count - 2)

    send_rim = remote(
        streams_hbm.at[:, pl.ds(tokens - 16, 16), :], rim, rim_sem.at[0], rim_sem.at[1],
        ctx_at(1), my_ch,
    )
    send_rim.start()

    def ch_copy(step):
        to = ch_at(step)
        return remote(
            chosen.at[to, 0], bank.at[my_ch, 0], ch_send.at[step], ch_recv.at[step], me, to
        )

    def ch_extra(step):
        to = ch_at(step)
        at = ch_count + step
        return remote(
            chosen.at[to, 1], bank.at[my_ch, 1], ch_send.at[at], ch_recv.at[at], me, to
        )

    for step in range(1, ch_count):
        ch_copy(step).start()

    @pl.when(me == 0)
    def _():
        for step in range(1, ch_count):
            ch_extra(step).start()

    for load in loads[3:5]:
        load.wait()
    send_rim.wait()
    chunk = 64

    def feature(stream, lanes, store):
        ext[0:8, :] = rim[stream, :, lanes].astype(f32)[8:16]
        ext[8 : 8 + tokens, :] = streams[stream, :, lanes].astype(f32)
        for at in range(0, tokens, chunk):
            where_in = inside[at : at + chunk, :]
            total = jnp.zeros((chunk, LANES), f32)
            for tap in range(FEAT_TAPS):
                term = taps[stream, tap : tap + 1, lanes] * ext[at + 8 - tap : at + 8 - tap + chunk, :]
                if tap:
                    term = jnp.where(where_in >= tap, term, 0.0)
                total = total + term
            store(at, total)

    def product(block):
        lanes = pl.ds(pl.multiple_of(block * LANES, LANES), LANES)

        def put_key(at, total):
            keep[block, at : at + chunk, :] = total

        def put_product(at, total):
            both = keep[block, at : at + chunk, :] * total
            keep[block, at : at + chunk, :] = both
            sends[block, at : at + chunk, :] = both.astype(bf16)

        feature(1, lanes, put_key)
        feature(2, lanes, put_product)

    def order(index):
        return 1 + lax.rem(index + 3, ctx_count - 1)

    def go_copy(step):
        to = ctx_at(step)
        return remote(sends.at[to], columns.at[me], go_send.at[step], go_recv.at[step], to, my_ch)

    def go(index, carry):
        step = order(index)
        product(ctx_at(step))
        go_copy(step).start()
        return carry

    lax.fori_loop(0, ctx_count - 1, go, 0)
    product(me)
    columns[me] = sends[me]

    for step in range(1, ch_count):
        ch_copy(step).wait()

    def add_picks(row):
        bank[my_ch, row] = chosen[my_ch, row]
        for c in range(ctx_count):
            total = bank[0, row, c].astype(f32)
            for h in range(1, ch_count):
                total = total + bank[h, row, c].astype(f32)
            mine[row, c] = total.astype(bf16)

    add_picks(0)

    def spec_copy(step):
        to = ctx_at(step)
        return remote(
            mine.at[0, to], spec.at[me], spec_send.at[step], spec_recv.at[step], to, my_ch
        )

    def last_copy(step):
        return remote(
            mine.at[1, step], spec.at[ctx_count], last_send.at[step], last_recv.at[0], step, my_ch
        )

    for step in range(1, ctx_count):
        spec_copy(step).start()
    spec[me] = mine[0, me]

    @pl.when(me == 0)
    def _():
        for step in range(1, ch_count):
            ch_extra(step).wait()
        add_picks(1)
        for step in range(1, ctx_count):
            last_copy(step).start()
        spec[ctx_count] = mine[1, 0]

    def ask(block, carry):
        lanes = pl.ds(pl.multiple_of(block * LANES, LANES), LANES)

        def put_query(at, total):
            query[block, at : at + chunk, :] = total

        feature(0, lanes, put_query)
        return carry

    lax.fori_loop(0, ctx_count, ask, 0)

    for load in loads[5:]:
        load.wait()
    for step in range(1, ctx_count):
        spec_copy(step).wait()

    @pl.when(me == 0)
    def _():
        for step in range(1, ctx_count):
            last_copy(step).wait_send()

    @pl.when(me != 0)
    def _():
        last_copy(1).wait_recv()

    lane = lax.broadcasted_iota(jnp.int32, (16, 2 * LANES), 1)
    owner = lane % LANES // GROUP_CH + lane // LANES * 8
    picking = lax.broadcasted_iota(jnp.int32, (16, 2 * LANES), 0) == owner
    spread = jnp.where(picking, 1.0, 0.0).astype(bf16)
    dft[...] = dft_wide[...].astype(bf16)

    def widen(k, carry):
        picked = spec[k].astype(f32).T.astype(bf16)
        wide[k] = jnp.dot(picked, spread, preferred_element_type=f32)
        return carry

    lax.fori_loop(0, ctx_count + 1, widen, 0)

    for step in range(1, ctx_count):
        go_copy(step).wait()

    half = ctx_count // 2
    rows = 16

    def co(a, k):
        return math.cos(math.pi * (a * k % (2 * ctx_count)) / ctx_count)

    def si(a, k):
        return math.sin(math.pi * (a * k % (2 * ctx_count)) / ctx_count)

    def gather(terms, coefs):
        total = None
        for term, coef in zip(terms, coefs):
            if abs(coef) < 1e-9:
                continue
            if abs(coef - 1) < 1e-9:
                piece = term
            elif abs(coef + 1) < 1e-9:
                piece = -term
            else:
                piece = term * coef
            total = piece if total is None else total + piece
        return jnp.zeros_like(terms[0]) if total is None else total

    def outer_step(index, carry):
        at = pl.ds(pl.multiple_of(index * rows, rows), rows)
        x = [columns[a, at, :].astype(f32) for a in range(ctx_count)]
        even, odd = list(range(0, ctx_count, 2)), list(range(1, ctx_count, 2))

        def put(k, real, imag):
            c, s = twist[k, 0, at, :], twist[k, 1, at, :]
            inner_in[k, at, 0:LANES] = (real * c + imag * s).astype(bf16)
            inner_in[k, at, LANES : 2 * LANES] = (imag * c - real * s).astype(bf16)

        for k in range(half + 1):
            ce = gather([x[a] for a in even], [co(a, k) for a in even])
            cd = gather([x[a] for a in odd], [co(a, k) for a in odd])
            se = gather([x[a] for a in even], [si(a, k) for a in even])
            sd = gather([x[a] for a in odd], [si(a, k) for a in odd])
            put(k, ce + cd, -(se + sd))
            if k != ctx_count - k:
                put(ctx_count - k, ce - cd, se - sd)
        return carry

    lax.fori_loop(0, tokens // rows, outer_step, 0)

    def inner(both):
        result = jnp.dot(dft[...], both, preferred_element_type=f32)
        return (
            result[:tokens, :LANES], result[:tokens, LANES:],
            result[tokens:, :LANES], result[tokens:, LANES:],
        )

    for k in range(ctx_count + 1):
        s_real, s_imag = wide[k, :, :LANES], wide[k, :, LANES:]
        cr, ci, sr, sj = inner(inner_in[k])
        z_real, z_imag = cr + sj, ci - sr
        inner_in[k, :, :LANES] = (z_real * s_real - z_imag * s_imag).astype(bf16)
        inner_in[k, :, LANES:] = (z_real * s_imag + z_imag * s_real).astype(bf16)

    for k in range(ctx_count + 1):
        cr, ci, sr, sj = inner(inner_in[k])
        v_real, v_imag = cr - sj, ci + sr
        c, s = twist[k, 0], twist[k, 1]
        inner_out[k, 0] = v_real * c - v_imag * s
        inner_out[k, 1] = v_imag * c + v_real * s

    def last_step(index, carry):
        at = pl.ds(pl.multiple_of(index * rows, rows), rows)
        real = [inner_out[k, 0, at, :] for k in range(ctx_count + 1)]
        imag = [inner_out[k, 1, at, :] for k in range(ctx_count + 1)]
        for parity in range(2):
            sign = 1.0 if parity == 0 else -1.0
            folded_r = [real[k] + sign * real[ctx_count - k] for k in range(half)] + [real[half]]
            folded_i = [imag[k] - sign * imag[ctx_count - k] for k in range(half)] + [imag[half]]
            for a in range(parity, ctx_count, 2):
                weights = [(1.0 if k == 0 else 2.0) for k in range(half + 1)]
                total = gather(
                    folded_r + folded_i,
                    [w * co(a, k) for k, w in enumerate(weights)]
                    + [-w * si(a, k) for k, w in enumerate(weights)],
                )
                signal[a, at, :] = (total * (1.0 / total_len)).astype(bf16)
        return carry

    lax.fori_loop(0, tokens // rows, last_step, 0)

    def back_copy(step):
        to = ctx_at(step)
        return remote(signal.at[to], back.at[me], back_send.at[step], back_recv.at[step], to, my_ch)

    def send_back(index, carry):
        back_copy(order(index)).start()
        return carry

    lax.fori_loop(0, ctx_count - 1, send_back, 0)

    def finish(block, conv):
        lanes = pl.ds(pl.multiple_of(block * LANES, LANES), LANES)
        skipped = gain[0:1, lanes] * keep[block]
        out[:, lanes] = (query[block] * (conv.astype(f32) + skipped)).astype(bf16)

    finish(me, signal[me])

    def receive(index, carry):
        step = order(index)
        back_copy(step).wait()
        source = lax.rem(me + ctx_count - step, ctx_count)
        finish(source, back[source])
        return carry

    lax.fori_loop(0, ctx_count - 1, receive, 0)


def fused(
    streams, feat_weight, skip_gain, spectrum_values, spectrum_scales, group_filter,
    doc_lengths
):
    ctx_count, ch_count = lax.axis_size("ctx"), lax.axis_size("ch")
    tokens, _, local_ch = streams.shape
    rows = ctx_count + 1
    f32, bf16 = jnp.float32, jnp.bfloat16
    cos_t, sin_t = wave(np.arange(rows), np.arange(tokens), 2 * tokens * ctx_count)
    twist = np.stack([cos_t, sin_t], axis=1).astype(np.float32)[..., None]
    twist = np.ascontiguousarray(np.broadcast_to(twist, twist.shape[:3] + (LANES,)))
    cos_i, sin_i = wave(np.arange(tokens), np.arange(tokens), tokens)
    dft = jnp.asarray(np.concatenate([cos_i, sin_i], axis=0), f32)
    vmem = pl.BlockSpec(memory_space=pltpu.VMEM)
    hbm = pl.BlockSpec(memory_space=pl.ANY)
    dma = lambda count: pltpu.SemaphoreType.DMA((count,))
    block = (ctx_count, tokens, LANES)
    picks = (2, ctx_count, 16, tokens)
    return pl.pallas_call(
        functools.partial(block_kernel, ctx_count, ch_count),
        out_shape=jax.ShapeDtypeStruct((tokens, local_ch), bf16),
        in_specs=[hbm, pl.BlockSpec(memory_space=pltpu.SMEM)] + [hbm] * 7,
        out_specs=vmem,
        scratch_shapes=[
            pltpu.VMEM((3, tokens, local_ch), bf16),
            pltpu.VMEM((tokens, LANES), jnp.int32),
            pltpu.VMEM(feat_weight.shape, f32),
            pltpu.VMEM((1, local_ch), f32),
            pltpu.VMEM(spectrum_values.shape, bf16),
            pltpu.VMEM(spectrum_scales.shape, f32),
            pltpu.VMEM((1,) + group_filter.shape, jnp.int32),
            pltpu.VMEM((2 * tokens, tokens), f32),
            pltpu.VMEM((2 * tokens, tokens), bf16),
            pltpu.VMEM((rows, 2, tokens, LANES), f32),
            pltpu.VMEM((rows, tokens, 2 * LANES), f32),
            pltpu.VMEM((tokens + 8, LANES), f32),
            pltpu.VMEM((3, 16, local_ch), bf16),
            pltpu.VMEM((ch_count,) + picks, bf16),
            pltpu.VMEM((ch_count,) + picks, bf16),
            pltpu.VMEM(picks, bf16),
            pltpu.VMEM((rows, 16, tokens), bf16),
            pltpu.VMEM(block, f32),
            pltpu.VMEM(block, f32),
            pltpu.VMEM(block, bf16),
            pltpu.VMEM(block, bf16),
            pltpu.VMEM((rows, tokens, 2 * LANES), bf16),
            pltpu.VMEM((rows, 2, tokens, LANES), f32),
            pltpu.VMEM(block, bf16),
            pltpu.VMEM(block, bf16),
            dma(8), dma(2), dma(2 * ch_count), dma(2 * ch_count), dma(ctx_count), dma(ctx_count),
            dma(ctx_count), dma(1), dma(ctx_count), dma(ctx_count), dma(ctx_count), dma(ctx_count),
        ],
        compiler_params=pltpu.CompilerParams(
            collective_id=0, has_side_effects=True, vmem_limit_bytes=56 * 2**20
        ),
    )(
        jnp.transpose(streams, (1, 0, 2)), doc_lengths, feat_weight, skip_gain[None],
        spectrum_values, spectrum_scales, group_filter[None], dft, jnp.asarray(twist),
    )


def per_device(
    streams, feat_weight, skip_gain, spectrum_values, spectrum_scales, group_filter, doc_lengths
):
    tokens, _, local_ch = streams.shape
    filters = spectrum_values.shape[3]
    if local_ch != lax.axis_size("ctx") * LANES or filters % LANES or tokens % SCALE_BLOCK:
        return by_collectives(
            streams, feat_weight, skip_gain, spectrum_values, spectrum_scales, group_filter,
            doc_lengths,
        )
    return fused(
        streams, feat_weight, skip_gain, spectrum_values, spectrum_scales, group_filter, doc_lengths
    )


def solution(mesh):
    placed = (
        P("ctx", None, "ch"),
        P(None, None, "ch"),
        P("ch"),
        P(None, "ctx", None, "ch"),
        P("ctx", None, "ch"),
        P(),
        P(),
    )
    return jax.shard_map(
        per_device, mesh=mesh, in_specs=placed, out_specs=P("ctx", "ch"), check_vma=False
    )
```

```python
import functools
import math

import jax
import jax.numpy as jnp
import numpy as np
from jax import lax
from jax.experimental import pallas as pl
from jax.experimental.pallas import tpu as pltpu
from jax.sharding import PartitionSpec as P

GROUP_CH = 16
FEAT_TAPS = 7
SCALE_BLOCK = 128


def from_behind(shard, axis, by):
    size = lax.axis_size(axis)
    pairs = [(i, i + by) for i in range(size) if 0 <= i + by < size]
    return lax.ppermute(shard, axis, pairs)


def wave(rows, cols, period):
    angle = np.outer(rows, cols) % period * (2.0 * math.pi / period)
    return np.cos(angle), np.sin(angle)


def featurize(streams, rim, feat_weight, doc_lengths, ctx_index):
    tokens = streams.shape[0]
    reach = FEAT_TAPS - 1
    extended = jnp.concatenate([rim, streams], axis=0).astype(jnp.float32)
    positions = ctx_index * tokens + jnp.arange(tokens, dtype=jnp.int32)
    ends = jnp.cumsum(doc_lengths)
    begins = jnp.max(jnp.where(positions[:, None] >= ends[None, :], ends[None, :], 0), axis=1)
    inside = positions - begins
    featured = jnp.zeros((tokens,) + streams.shape[1:], jnp.float32)
    for tap_index in range(FEAT_TAPS):
        start = reach - tap_index
        source = extended[start : start + tokens]
        same = inside >= tap_index
        featured = featured + jnp.where(
            same[:, None, None], feat_weight[:, tap_index, :][None] * source, 0.0
        )
    return featured[:, 0], featured[:, 1] * featured[:, 2]


def long_conv(columns, spec_real, spec_imag, ctx_count):
    tokens = columns.shape[1]
    total_len = 2 * tokens * ctx_count
    outer = np.arange(ctx_count + 1)
    cos_o, sin_o = wave(outer, np.arange(ctx_count), 2 * ctx_count)
    cos_t, sin_t = wave(outer, np.arange(tokens), total_len)
    cos_i, sin_i = wave(np.arange(tokens), np.arange(tokens), tokens)
    f32 = jnp.float32
    high = lax.Precision.HIGHEST
    xs = columns.astype(f32)
    u_real = jnp.einsum("ka,abc->kbc", jnp.asarray(cos_o, f32), xs, precision=high)
    u_imag = jnp.einsum("ka,abc->kbc", jnp.asarray(-sin_o, f32), xs, precision=high)
    ct, st = jnp.asarray(cos_t, f32)[:, :, None], jnp.asarray(sin_t, f32)[:, :, None]
    b_real = (u_real * ct + u_imag * st).astype(jnp.bfloat16)
    b_imag = (u_imag * ct - u_real * st).astype(jnp.bfloat16)
    table = jnp.asarray(np.concatenate([cos_i, sin_i], axis=0), jnp.bfloat16)

    def inner(real, imag):
        both = jnp.concatenate([real, imag], axis=2)
        out = jnp.einsum("qt,ktc->kqc", table, both, preferred_element_type=f32)
        width = real.shape[2]
        return (
            out[:, :tokens, :width],
            out[:, :tokens, width:],
            out[:, tokens:, :width],
            out[:, tokens:, width:],
        )

    cr, ci, sr, si = inner(b_real, b_imag)
    z_real, z_imag = cr + si, ci - sr
    p_real = (z_real * spec_real - z_imag * spec_imag).astype(jnp.bfloat16)
    p_imag = (z_real * spec_imag + z_imag * spec_real).astype(jnp.bfloat16)
    cr, ci, sr, si = inner(p_real, p_imag)
    v_real, v_imag = cr - si, ci + sr
    t_real = v_real * ct - v_imag * st
    t_imag = v_imag * ct + v_real * st
    weight = np.where((outer == 0) | (outer == ctx_count), 1.0, 2.0)[:, None] / total_len
    back_r = jnp.asarray(cos_o * weight, f32)
    back_i = jnp.asarray(-sin_o * weight, f32)
    return jnp.einsum("ka,kbc->abc", back_r, t_real, precision=high) + jnp.einsum(
        "ka,kbc->abc", back_i, t_imag, precision=high
    )


def by_collectives(
    streams, feat_weight, skip_gain, spectrum_values, spectrum_scales, group_filter, doc_lengths
):
    tokens = streams.shape[0]
    local_ch = streams.shape[2]
    ctx_count = lax.axis_size("ctx")
    reach = FEAT_TAPS - 1
    ctx_index = lax.axis_index("ctx")
    ch_index = lax.axis_index("ch")
    groups_local = local_ch // GROUP_CH
    scaled = spectrum_values.astype(jnp.float32) * jnp.repeat(spectrum_scales, SCALE_BLOCK, axis=1)
    bank = lax.all_gather(scaled.astype(jnp.bfloat16), "ch", axis=3, tiled=True)
    mine = lax.dynamic_slice_in_dim(group_filter, ch_index * groups_local, groups_local)
    onehot = jnp.arange(bank.shape[3], dtype=jnp.int32)[:, None] == mine[None, :]
    chosen = jnp.einsum(
        "rkqf,fg->kgrq", bank, onehot.astype(jnp.bfloat16), preferred_element_type=jnp.float32
    ).astype(jnp.bfloat16)
    rim = from_behind(streams[tokens - reach :], "ctx", 1)
    query, mixed_in = featurize(streams, rim, feat_weight, doc_lengths, ctx_index)
    columns = lax.all_to_all(
        mixed_in.astype(jnp.bfloat16), "ctx", split_axis=1, concat_axis=0, tiled=True
    ).reshape(ctx_count, tokens, -1)
    spec = lax.all_to_all(chosen, "ctx", split_axis=1, concat_axis=0, tiled=True)
    spec = jnp.concatenate([spec[0::2], spec[1:2]], axis=0)
    spec = jnp.repeat(jnp.transpose(spec, (2, 0, 3, 1)), GROUP_CH, axis=3).astype(jnp.float32)
    signal = long_conv(columns, spec[0], spec[1], ctx_count)
    conv = lax.all_to_all(
        signal.astype(jnp.bfloat16), "ctx", split_axis=0, concat_axis=2, tiled=True
    ).reshape(tokens, local_ch)
    conv = conv.astype(jnp.float32)
    return (query * (conv + skip_gain[None] * mixed_in)).astype(jnp.bfloat16)


LANES = 128


def block_kernel(
    ctx_count, ch_count,
    streams_hbm, lengths, taps_hbm, gain_hbm, values_hbm, scales_hbm, groups_hbm, dft_hbm,
    twist_hbm,
    out,
    streams, inside, taps, gain, values, scales, groups, dft_wide, dft, twist, wide, ext, rim, chosen, bank, mine, spec, keep, query, sends, columns,
    inner_in, inner_out, signal, back,
    table_sem, rim_sem, ch_send, ch_recv, spec_send, spec_recv, last_send, last_recv,
    go_send, go_recv, back_send, back_recv,
):
    f32, bf16 = jnp.float32, jnp.bfloat16
    tokens = streams_hbm.shape[1]
    me = lax.axis_index("ctx")
    my_ch = lax.axis_index("ch")
    total_len = 2 * tokens * ctx_count

    def remote(src, dst, send, recv, ctx_to, ch_to):
        return pltpu.make_async_remote_copy(
            src_ref=src, dst_ref=dst, send_sem=send, recv_sem=recv,
            device_id=(ctx_to, ch_to), device_id_type=pl.DeviceIdType.MESH,
        )

    def ctx_at(step):
        return lax.rem(me + step, ctx_count)

    def ch_at(step):
        return lax.rem(my_ch + step, ch_count)

    loads = [
        pltpu.make_async_copy(source, target, table_sem.at[index])
        for index, (source, target) in enumerate(
            [
                (values_hbm, values), (scales_hbm, scales), (groups_hbm, groups),
                (taps_hbm, taps), (streams_hbm, streams),
                (gain_hbm, gain), (dft_hbm, dft_wide), (twist_hbm, twist),
            ]
        )
    ]
    for load in loads:
        load.start()

    barrier = pltpu.get_barrier_semaphore()
    for step in range(1, ctx_count):
        pl.semaphore_signal(
            barrier, inc=1, device_id=(ctx_at(step), my_ch), device_id_type=pl.DeviceIdType.MESH
        )
    for step in range(1, ch_count):
        pl.semaphore_signal(
            barrier, inc=1, device_id=(me, ch_at(step)), device_id_type=pl.DeviceIdType.MESH
        )

    begins = jnp.zeros((tokens, LANES), jnp.int32)
    places = me * tokens + lax.broadcasted_iota(jnp.int32, (tokens, LANES), 0)
    end = jnp.int32(0)
    for doc in range(lengths.shape[0]):
        end = end + lengths[doc]
        begins = jnp.where(places >= end, end, begins)
    inside[...] = places - begins

    pl.semaphore_wait(barrier, ctx_count + ch_count - 2)

    send_rim = remote(
        streams_hbm.at[:, pl.ds(tokens - 16, 16), :], rim, rim_sem.at[0], rim_sem.at[1],
        ctx_at(1), my_ch,
    )
    send_rim.start()

    for load in loads[:3]:
        load.wait()
    filters = values.shape[3]
    held = my_ch * filters + lax.broadcasted_iota(jnp.int32, (filters, groups.shape[1]), 0)
    onehot = jnp.where(held == groups[...], 1.0, 0.0).astype(f32).T.astype(bf16)
    halves = tokens // SCALE_BLOCK
    for row in range(2):
        parts = []
        for part in range(2):
            bands = []
            for half in range(halves):
                band = values[part, row, half * SCALE_BLOCK : (half + 1) * SCALE_BLOCK, :]
                bands.append(band.astype(f32) * scales[row, half : half + 1, :])
            scaled = jnp.concatenate(bands, axis=0).astype(bf16)
            parts.append(
                lax.dot_general(
                    onehot, scaled, (((1,), (1,)), ((), ())), preferred_element_type=f32
                )
            )
        for h in range(ch_count):
            for c in range(ctx_count):
                at = (h * ctx_count + c) * 8
                chosen[h, row, c] = jnp.concatenate(
                    [parts[0][at : at + 8], parts[1][at : at + 8]], axis=0
                ).astype(bf16)

    def ch_copy(step):
        to = ch_at(step)
        return remote(
            chosen.at[to, 0], bank.at[my_ch, 0], ch_send.at[step], ch_recv.at[step], me, to
        )

    def ch_extra(step):
        to = ch_at(step)
        at = ch_count + step
        return remote(
            chosen.at[to, 1], bank.at[my_ch, 1], ch_send.at[at], ch_recv.at[at], me, to
        )

    for step in range(1, ch_count):
        ch_copy(step).start()

    @pl.when(me == 0)
    def _():
        for step in range(1, ch_count):
            ch_extra(step).start()

    for load in loads[3:5]:
        load.wait()
    send_rim.wait()
    chunk = 64

    def feature(stream, lanes, store):
        ext[0:8, :] = rim[stream, :, lanes].astype(f32)[8:16]
        ext[8 : 8 + tokens, :] = streams[stream, :, lanes].astype(f32)
        for at in range(0, tokens, chunk):
            where_in = inside[at : at + chunk, :]
            total = jnp.zeros((chunk, LANES), f32)
            for tap in range(FEAT_TAPS):
                term = taps[stream, tap : tap + 1, lanes] * ext[at + 8 - tap : at + 8 - tap + chunk, :]
                if tap:
                    term = jnp.where(where_in >= tap, term, 0.0)
                total = total + term
            store(at, total)

    def product(block):
        lanes = pl.ds(pl.multiple_of(block * LANES, LANES), LANES)

        def put_key(at, total):
            keep[block, at : at + chunk, :] = total

        def put_product(at, total):
            both = keep[block, at : at + chunk, :] * total
            keep[block, at : at + chunk, :] = both
            sends[block, at : at + chunk, :] = both.astype(bf16)

        feature(1, lanes, put_key)
        feature(2, lanes, put_product)

    def order(index):
        return 1 + index

    def go_copy(step):
        to = ctx_at(step)
        return remote(sends.at[to], columns.at[me], go_send.at[step], go_recv.at[step], to, my_ch)

    def go(index, carry):
        step = order(index)
        product(ctx_at(step))
        go_copy(step).start()
        return carry

    lax.fori_loop(0, ctx_count - 1, go, 0)
    product(me)
    columns[me] = sends[me]

    for step in range(1, ch_count):
        ch_copy(step).wait()

    def add_picks(row):
        bank[my_ch, row] = chosen[my_ch, row]
        for c in range(ctx_count):
            total = bank[0, row, c].astype(f32)
            for h in range(1, ch_count):
                total = total + bank[h, row, c].astype(f32)
            mine[row, c] = total.astype(bf16)

    add_picks(0)

    def spec_copy(step):
        to = ctx_at(step)
        return remote(
            mine.at[0, to], spec.at[me], spec_send.at[step], spec_recv.at[step], to, my_ch
        )

    def last_copy(step):
        return remote(
            mine.at[1, step], spec.at[ctx_count], last_send.at[step], last_recv.at[0], step, my_ch
        )

    for step in range(1, ctx_count):
        spec_copy(step).start()
    spec[me] = mine[0, me]

    @pl.when(me == 0)
    def _():
        for step in range(1, ch_count):
            ch_extra(step).wait()
        add_picks(1)
        for step in range(1, ctx_count):
            last_copy(step).start()
        spec[ctx_count] = mine[1, 0]

    def ask(block, carry):
        lanes = pl.ds(pl.multiple_of(block * LANES, LANES), LANES)

        def put_query(at, total):
            query[block, at : at + chunk, :] = total

        feature(0, lanes, put_query)
        return carry

    lax.fori_loop(0, ctx_count, ask, 0)

    for load in loads[5:]:
        load.wait()
    for step in range(1, ctx_count):
        spec_copy(step).wait()

    @pl.when(me == 0)
    def _():
        for step in range(1, ctx_count):
            last_copy(step).wait_send()

    @pl.when(me != 0)
    def _():
        last_copy(1).wait_recv()

    lane = lax.broadcasted_iota(jnp.int32, (16, 2 * LANES), 1)
    owner = lane % LANES // GROUP_CH + lane // LANES * 8
    picking = lax.broadcasted_iota(jnp.int32, (16, 2 * LANES), 0) == owner
    spread = jnp.where(picking, 1.0, 0.0).astype(bf16)
    dft[...] = dft_wide[...].astype(bf16)

    def widen(k, carry):
        picked = spec[k].astype(f32).T.astype(bf16)
        wide[k] = jnp.dot(picked, spread, preferred_element_type=f32)
        return carry

    lax.fori_loop(0, ctx_count + 1, widen, 0)

    for step in range(1, ctx_count):
        go_copy(step).wait()

    half = ctx_count // 2
    rows = 16

    def co(a, k):
        return math.cos(math.pi * (a * k % (2 * ctx_count)) / ctx_count)

    def si(a, k):
        return math.sin(math.pi * (a * k % (2 * ctx_count)) / ctx_count)

    def gather(terms, coefs):
        total = None
        for term, coef in zip(terms, coefs):
            if abs(coef) < 1e-9:
                continue
            if abs(coef - 1) < 1e-9:
                piece = term
            elif abs(coef + 1) < 1e-9:
                piece = -term
            else:
                piece = term * coef
            total = piece if total is None else total + piece
        return jnp.zeros_like(terms[0]) if total is None else total

    def outer_step(index, carry):
        at = pl.ds(pl.multiple_of(index * rows, rows), rows)
        x = [columns[a, at, :].astype(f32) for a in range(ctx_count)]
        even, odd = list(range(0, ctx_count, 2)), list(range(1, ctx_count, 2))

        def put(k, real, imag):
            c, s = twist[k, 0, at, :], twist[k, 1, at, :]
            inner_in[k, at, 0:LANES] = (real * c + imag * s).astype(bf16)
            inner_in[k, at, LANES : 2 * LANES] = (imag * c - real * s).astype(bf16)

        for k in range(half + 1):
            ce = gather([x[a] for a in even], [co(a, k) for a in even])
            cd = gather([x[a] for a in odd], [co(a, k) for a in odd])
            se = gather([x[a] for a in even], [si(a, k) for a in even])
            sd = gather([x[a] for a in odd], [si(a, k) for a in odd])
            put(k, ce + cd, -(se + sd))
            if k != ctx_count - k:
                put(ctx_count - k, ce - cd, se - sd)
        return carry

    lax.fori_loop(0, tokens // rows, outer_step, 0)

    def inner(both):
        result = jnp.dot(dft[...], both, preferred_element_type=f32)
        return (
            result[:tokens, :LANES], result[:tokens, LANES:],
            result[tokens:, :LANES], result[tokens:, LANES:],
        )

    for k in range(ctx_count + 1):
        s_real, s_imag = wide[k, :, :LANES], wide[k, :, LANES:]
        cr, ci, sr, sj = inner(inner_in[k])
        z_real, z_imag = cr + sj, ci - sr
        inner_in[k, :, :LANES] = (z_real * s_real - z_imag * s_imag).astype(bf16)
        inner_in[k, :, LANES:] = (z_real * s_imag + z_imag * s_real).astype(bf16)

    for k in range(ctx_count + 1):
        cr, ci, sr, sj = inner(inner_in[k])
        v_real, v_imag = cr - sj, ci + sr
        c, s = twist[k, 0], twist[k, 1]
        inner_out[k, 0] = v_real * c - v_imag * s
        inner_out[k, 1] = v_imag * c + v_real * s

    def last_step(index, carry):
        at = pl.ds(pl.multiple_of(index * rows, rows), rows)
        real = [inner_out[k, 0, at, :] for k in range(ctx_count + 1)]
        imag = [inner_out[k, 1, at, :] for k in range(ctx_count + 1)]
        for parity in range(2):
            sign = 1.0 if parity == 0 else -1.0
            folded_r = [real[k] + sign * real[ctx_count - k] for k in range(half)] + [real[half]]
            folded_i = [imag[k] - sign * imag[ctx_count - k] for k in range(half)] + [imag[half]]
            for a in range(parity, ctx_count, 2):
                weights = [(1.0 if k == 0 else 2.0) for k in range(half + 1)]
                total = gather(
                    folded_r + folded_i,
                    [w * co(a, k) for k, w in enumerate(weights)]
                    + [-w * si(a, k) for k, w in enumerate(weights)],
                )
                signal[a, at, :] = (total * (1.0 / total_len)).astype(bf16)
        return carry

    lax.fori_loop(0, tokens // rows, last_step, 0)

    def back_copy(step):
        to = ctx_at(step)
        return remote(signal.at[to], back.at[me], back_send.at[step], back_recv.at[step], to, my_ch)

    def send_back(index, carry):
        back_copy(order(index)).start()
        return carry

    lax.fori_loop(0, ctx_count - 1, send_back, 0)

    def finish(block, conv):
        lanes = pl.ds(pl.multiple_of(block * LANES, LANES), LANES)
        skipped = gain[0:1, lanes] * keep[block]
        out[:, lanes] = (query[block] * (conv.astype(f32) + skipped)).astype(bf16)

    finish(me, signal[me])

    def receive(index, carry):
        step = order(index)
        back_copy(step).wait()
        source = lax.rem(me + ctx_count - step, ctx_count)
        finish(source, back[source])
        return carry

    lax.fori_loop(0, ctx_count - 1, receive, 0)


def fused(
    streams, feat_weight, skip_gain, spectrum_values, spectrum_scales, group_filter,
    doc_lengths
):
    ctx_count, ch_count = lax.axis_size("ctx"), lax.axis_size("ch")
    tokens, _, local_ch = streams.shape
    rows = ctx_count + 1
    f32, bf16 = jnp.float32, jnp.bfloat16
    cos_t, sin_t = wave(np.arange(rows), np.arange(tokens), 2 * tokens * ctx_count)
    twist = np.stack([cos_t, sin_t], axis=1).astype(np.float32)[..., None]
    twist = np.ascontiguousarray(np.broadcast_to(twist, twist.shape[:3] + (LANES,)))
    cos_i, sin_i = wave(np.arange(tokens), np.arange(tokens), tokens)
    dft = jnp.asarray(np.concatenate([cos_i, sin_i], axis=0), f32)
    vmem = pl.BlockSpec(memory_space=pltpu.VMEM)
    hbm = pl.BlockSpec(memory_space=pl.ANY)
    dma = lambda count: pltpu.SemaphoreType.DMA((count,))
    block = (ctx_count, tokens, LANES)
    picks = (2, ctx_count, 16, tokens)
    return pl.pallas_call(
        functools.partial(block_kernel, ctx_count, ch_count),
        out_shape=jax.ShapeDtypeStruct((tokens, local_ch), bf16),
        in_specs=[hbm, pl.BlockSpec(memory_space=pltpu.SMEM)] + [hbm] * 7,
        out_specs=vmem,
        scratch_shapes=[
            pltpu.VMEM((3, tokens, local_ch), bf16),
            pltpu.VMEM((tokens, LANES), jnp.int32),
            pltpu.VMEM(feat_weight.shape, f32),
            pltpu.VMEM((1, local_ch), f32),
            pltpu.VMEM(spectrum_values.shape, bf16),
            pltpu.VMEM(spectrum_scales.shape, f32),
            pltpu.VMEM((1,) + group_filter.shape, jnp.int32),
            pltpu.VMEM((2 * tokens, tokens), f32),
            pltpu.VMEM((2 * tokens, tokens), bf16),
            pltpu.VMEM((rows, 2, tokens, LANES), f32),
            pltpu.VMEM((rows, tokens, 2 * LANES), f32),
            pltpu.VMEM((tokens + 8, LANES), f32),
            pltpu.VMEM((3, 16, local_ch), bf16),
            pltpu.VMEM((ch_count,) + picks, bf16),
            pltpu.VMEM((ch_count,) + picks, bf16),
            pltpu.VMEM(picks, bf16),
            pltpu.VMEM((rows, 16, tokens), bf16),
            pltpu.VMEM(block, f32),
            pltpu.VMEM(block, f32),
            pltpu.VMEM(block, bf16),
            pltpu.VMEM(block, bf16),
            pltpu.VMEM((rows, tokens, 2 * LANES), bf16),
            pltpu.VMEM((rows, 2, tokens, LANES), f32),
            pltpu.VMEM(block, bf16),
            pltpu.VMEM(block, bf16),
            dma(8), dma(2), dma(2 * ch_count), dma(2 * ch_count), dma(ctx_count), dma(ctx_count),
            dma(ctx_count), dma(1), dma(ctx_count), dma(ctx_count), dma(ctx_count), dma(ctx_count),
        ],
        compiler_params=pltpu.CompilerParams(
            collective_id=0, has_side_effects=True, vmem_limit_bytes=56 * 2**20
        ),
    )(
        jnp.transpose(streams, (1, 0, 2)), doc_lengths, feat_weight, skip_gain[None],
        spectrum_values, spectrum_scales, group_filter[None], dft, jnp.asarray(twist),
    )


def per_device(
    streams, feat_weight, skip_gain, spectrum_values, spectrum_scales, group_filter, doc_lengths
):
    tokens, _, local_ch = streams.shape
    filters = spectrum_values.shape[3]
    if local_ch != lax.axis_size("ctx") * LANES or filters % LANES or tokens % SCALE_BLOCK:
        return by_collectives(
            streams, feat_weight, skip_gain, spectrum_values, spectrum_scales, group_filter,
            doc_lengths,
        )
    return fused(
        streams, feat_weight, skip_gain, spectrum_values, spectrum_scales, group_filter, doc_lengths
    )


def solution(mesh):
    placed = (
        P("ctx", None, "ch"),
        P(None, None, "ch"),
        P("ch"),
        P(None, "ctx", None, "ch"),
        P("ctx", None, "ch"),
        P(),
        P(),
    )
    return jax.shard_map(
        per_device, mesh=mesh, in_specs=placed, out_specs=P("ctx", "ch"), check_vma=False
    )
```
